32 devices in a mesh: dp: 4 (over z), mp: 4 (over y, x), section: 2 (over core).
Axes of the slice: x: 2, y: 2, z: 4, core: 2. Of those that a mesh axis runs over, the one named last changes fastest.
Arguments:
- text_embeds: bfloat16 [3072, 8192], P('dp', 'mp')
- image_rows: bfloat16 [1536, 8192], P('dp', ('mp', 'section'))
- image_source: int32 [3072], P('dp'), may hold values from -1 to 1535, as said below
- live_len: int32 [4], P('dp'), may hold values from 192 to 768, as said below
- norm_gain: bfloat16 [8192], P(('mp', 'section')), may hold values from 0.25 to 1.75
Outputs:
- hessian: float32 [8192, 8192], P('dp', ('mp', 'section'))
The draws below stay inside these ranges and needn't reach their ends.
Inputs may be any that keep to these rules, and one draw needn't show every extreme that they name: `image_source`: every image row is placed at exactly one token; the tokens of each index of dp hold exactly 384 image rows, and at most 192 of them come from the image rows of any one index of dp, exactly 192 for some pairs in every draw. `live_len`: some index of dp has no padding in every draw.
All inputs are finite; a program needn't handle non-finite values.
Results may differ from the reference program's by a relative error of at most 0.008.
Values may be sent and summed in bfloat16 or wider, within the bound.
A program may use at most 128 MiB of HBM per device.

```python
import math
import jax
import jax.numpy as jnp
from jax import lax

D = 8192
TOK_DEV = 768
IMG_DEV = 384
TOKENS = 3072
IMAGES = 1536
N_DP = 4


def common_traits(key):
    key_a, key_b = jax.random.split(key, 2)
    shifts = jax.random.randint(key_a, (2,), 1, D)
    feature_scale = jnp.exp(jax.random.uniform(key_b, (D,), minval=0.0, maxval=math.log(10.0)))
    return (shifts, feature_scale)


def mix_rows(noise, key, shifts, feature_scale):
    row_count = noise.shape[0]
    row_scale = jnp.exp(jax.random.uniform(key, (row_count, 1), minval=math.log(0.5), maxval=math.log(4.0)))
    mixed = noise + 0.7 * jnp.roll(noise, shifts[0], axis=1) + 0.5 * jnp.roll(noise, shifts[1], axis=1)
    return mixed * feature_scale[None, :] * row_scale


def draw_text_embeds(key, part):
    shifts, feature_scale = common_traits(key)
    key = jax.random.fold_in(key, 5)
    key_a, key_b = jax.random.split(key)
    noise = jax.random.normal(key_a, (TOKENS, D))
    return mix_rows(noise, key_b, shifts, feature_scale).astype(jnp.bfloat16)


def draw_image_rows(key, part):
    shifts, feature_scale = common_traits(key)
    key = jax.random.fold_in(key, 6)
    key_a, key_b = jax.random.split(key)
    noise = jax.random.normal(key_a, (IMAGES, D))
    return mix_rows(noise, key_b, shifts, feature_scale).astype(jnp.bfloat16)


def draw_image_source(key, part):
    key = jax.random.fold_in(key, 7)
    key_a, key_b, key_c, key_d = jax.random.split(key, 4)
    base = IMG_DEV // N_DP
    half_count = N_DP // 2
    spread = jax.random.randint(key_a, (half_count,), 0, base + 1).at[0].set(base)
    loads = jnp.concatenate([base + spread, base - spread])
    loads = loads[jax.random.permutation(key_b, N_DP)]
    bounds = jnp.cumsum(loads)
    entry = jnp.arange(IMG_DEV, dtype=jnp.int32)
    block = jnp.sum((entry[:, None] >= bounds[None, :]).astype(jnp.int32), axis=1)
    row_perms = jax.vmap(lambda one_key: jax.random.permutation(one_key, IMG_DEV))(jax.random.split(key_c, N_DP))
    dest = jnp.arange(N_DP, dtype=jnp.int32)[:, None]
    source = (dest + block[None, :]) % N_DP
    local_row = row_perms[source, entry[None, :]]
    global_row = (source * IMG_DEV + local_row).astype(jnp.int32)
    slots = jax.vmap(lambda one_key: jax.random.permutation(one_key, TOK_DEV))(jax.random.split(key_d, N_DP))[:, :IMG_DEV]
    placed = jax.vmap(lambda slot_ids, rows: jnp.full((TOK_DEV,), -1, jnp.int32).at[slot_ids].set(rows))(slots, global_row)
    return placed.reshape(TOKENS).astype(jnp.int32)


def draw_live_len(key, part):
    key = jax.random.fold_in(key, 8)
    key_a, key_b = jax.random.split(key)
    lengths = jax.random.randint(key_a, (N_DP,), TOK_DEV // 4, TOK_DEV + 1)
    chosen = jax.random.randint(key_b, (), 0, N_DP)
    return lengths.at[chosen].set(TOK_DEV).astype(jnp.int32)


def setup_inputs(seed: int = 0) -> dict:
    arg_keys = jax.random.split(jax.random.key(seed), 6)
    text_embeds = draw_text_embeds(jax.random.fold_in(arg_keys[5], 71), 0)
    image_rows = draw_image_rows(jax.random.fold_in(arg_keys[5], 71), 0)
    image_source = draw_image_source(jax.random.fold_in(arg_keys[5], 71), 0)
    live_len = draw_live_len(jax.random.fold_in(arg_keys[5], 71), 0)
    norm_gain = jnp.clip(1.0 + 0.15 * jax.random.normal(arg_keys[4], (D,), jnp.float32), 0.25, 1.75).astype(jnp.bfloat16)
    return {"text_embeds": text_embeds, "image_rows": image_rows, "image_source": image_source, "live_len": live_len, "norm_gain": norm_gain}


def reference(text_embeds, image_rows, image_source, live_len, norm_gain):
    is_image = image_source >= 0
    picked = image_rows[jnp.where(is_image, image_source, 0)]
    joined = jnp.where(is_image[:, None], picked, text_embeds)
    position = jnp.arange(TOKENS, dtype=jnp.int32)
    live_mask = (position % TOK_DEV < live_len[position // TOK_DEV]).astype(jnp.float32)
    widened = joined.astype(jnp.float32)
    inverse = lax.rsqrt(lax.optimization_barrier(jnp.mean(widened * widened, axis=1, keepdims=True)) + 1e-06)
    normed = (widened * inverse * norm_gain.astype(jnp.float32)[None, :] * live_mask[:, None]).astype(jnp.bfloat16)
    group_rows = normed.reshape(N_DP, TOK_DEV, D)

    def add_group(total, block_rows):
        rows_wide = block_rows.astype(jnp.float32)
        partial_value = lax.dot_general(rows_wide, rows_wide, (((0,), (0,)), ((), ())), precision=lax.Precision.HIGHEST, preferred_element_type=jnp.float32)
        rounded = lax.optimization_barrier(partial_value.astype(jnp.bfloat16))
        return (total + rounded.astype(jnp.float32), None)
    total, _ = lax.scan(add_group, jnp.zeros((D, D), jnp.float32), group_rows)
    live_count = jnp.sum(live_mask)
    return total * (2.0 / live_count)
```

```python
import functools

import jax
import jax.numpy as jnp
from jax import lax
from jax.experimental import pallas as pl
from jax.experimental.pallas import tpu as pltpu
from jax.sharding import PartitionSpec as P

NORM_EPS = 1e-06
MESH = pl.DeviceIdType.MESH
CHUNK = 128
GROUP = 256
LANES = 128
TILE = 256


def general_body(text_embeds, image_rows, image_source, live_len, norm_gain):
    group_count = lax.axis_size("dp")
    feature_groups = lax.axis_size(("mp", "section"))
    tok_rows = text_embeds.shape[0]
    image_count = image_rows.shape[0]
    narrow = image_rows.shape[1]
    capacity = 2 * image_count // group_count
    section_part = lax.axis_index("section")
    own_text = lax.dynamic_slice_in_dim(text_embeds, section_part * narrow, narrow, 1)
    is_image = image_source >= 0
    safe_src = jnp.where(is_image, image_source, 0)
    owner_dev = safe_src // image_count
    local_row = safe_src % image_count
    peer_ids = jnp.arange(group_count, dtype=jnp.int32)
    onehot = ((owner_dev[:, None] == peer_ids[None, :]) & is_image[:, None]).astype(jnp.int32)
    slot_rank = jnp.sum(jnp.cumsum(onehot, axis=0) * onehot, axis=1) - 1
    empty_table = jnp.full((group_count * capacity,), -1, jnp.int32)
    wanted = jnp.where(is_image, owner_dev * capacity + slot_rank, group_count * capacity)
    request_table = empty_table.at[wanted].set(local_row, mode="drop")
    asked_rows = lax.all_to_all(
        request_table.reshape(group_count, capacity), "dp", split_axis=0, concat_axis=0, tiled=True
    )
    is_valid = asked_rows >= 0
    outgoing = image_rows[jnp.where(is_valid, asked_rows, 0)] * is_valid[:, :, None].astype(
        jnp.bfloat16
    )
    incoming = lax.all_to_all(outgoing, "dp", split_axis=0, concat_axis=0, tiled=True)
    wanted_slot = jnp.where(is_image, owner_dev * capacity + slot_rank, 0)
    picked = incoming.reshape(group_count * capacity, narrow)[wanted_slot]
    joined = jnp.where(is_image[:, None], picked, own_text)
    live_mask = (jnp.arange(tok_rows) < live_len[0]).astype(jnp.float32)[:, None]
    widened = joined.astype(jnp.float32)
    squares = lax.psum(jnp.sum(widened * widened, axis=1), ("mp", "section"))
    inverse = lax.rsqrt(squares / (narrow * feature_groups) + NORM_EPS)
    own_cols = (
        widened * inverse[:, None] * norm_gain.astype(jnp.float32)[None, :] * live_mask
    ).astype(jnp.bfloat16)
    contract = (((0,), (0,)), ((), ()))
    all_cols = lax.all_gather(own_cols, ("mp", "section"), axis=1, tiled=True)
    summed = lax.psum_scatter(
        lax.dot_general(all_cols, own_cols, contract, preferred_element_type=jnp.float32).astype(
            jnp.bfloat16
        ),
        "dp",
        scatter_dimension=0,
        tiled=True,
    ).astype(jnp.float32)
    live_count = lax.psum(jnp.sum(live_mask), "dp")
    return summed * (2.0 / live_count)


def ring_pos(m):
    y, x = m // 2, m % 2
    return y * (3 - x) + (1 - y) * x


def ring_chip(pos):
    y = pos // 2
    return 2 * y + (pos + y) % 2


def loop(count, step):
    lax.fori_loop(0, count, lambda i, carry: (step(i), carry)[1], 0)


def hessian_kernel(
    groups, text_ref, image_ref, code_ref, gain_ref, acc_ref, row_gain_ref,
    cols, rows, staged, codes, facts, w_row, w_col, scaled,
    load_sem, right_send, left_send, z_recv, ring_send, ring_recv, sib_send, sib_recv, own_sem,
    code_send, code_recv, fact_send, fact_recv, w_send, w_recv,
):
    g, m, s = lax.axis_index("dp"), lax.axis_index("mp"), lax.axis_index("section")
    images, narrow = image_ref.shape
    tokens = cols.shape[1]
    texts = tokens - images
    per = tokens // CHUNK
    members = facts.shape[0]
    me = m * 2 + s
    features = members * narrow
    turn = 1 - 2 * s
    here = ring_pos(m)
    hop = ((here - ring_pos(g)) * turn + 4) % 4
    next_chip = ring_chip((here + turn + 4) % 4)

    def chunk(ref, b, c):
        return ref.at[b, pl.ds(pl.multiple_of(c * CHUNK, CHUNK), CHUNK)]

    def remote(src, dst, send, recv, target):
        return pltpu.make_async_remote_copy(
            src_ref=src, dst_ref=dst, send_sem=send, recv_sem=recv,
            device_id=target, device_id_type=MESH,
        )

    def to_right(b, c):
        return remote(chunk(cols, b, c), chunk(cols, b, c), right_send.at[b * per + c],
                      z_recv.at[b * per + c], {"dp": lax.rem(g + 1, groups)})

    def to_left(b, c):
        return remote(chunk(cols, b, c), chunk(cols, b, c), left_send.at[b * per + c],
                      z_recv.at[b * per + c], {"dp": lax.rem(g + groups - 1, groups)})

    def round_ring(src, b, c):
        return remote(chunk(src, b, c), chunk(rows.at[s], b, c), ring_send.at[b * per + c],
                      ring_recv.at[b * per + c], {"mp": next_chip})

    def to_sibling(src, b, c, half):
        return remote(chunk(src, b, c), chunk(rows.at[half], b, c), sib_send.at[b * per + c],
                      sib_recv.at[b * per + c], {"section": 1 - s})

    def keep_own(b, c):
        return pltpu.make_async_copy(
            chunk(cols, b, c), chunk(rows.at[s], b, c), own_sem.at[b * per + c])

    def send_code(i):
        other = lax.rem(g + 1 + i, groups)
        return remote(code_ref, codes.at[g], code_send.at[i], code_recv.at[g], {"dp": other})

    def got_code(b):
        return remote(code_ref, codes.at[b], code_send.at[0], code_recv.at[b], {"dp": b})

    def send_w(i):
        other = lax.rem(g + 1 + i, groups)
        return remote(w_row.at[g], w_row.at[g], w_send.at[i], w_recv.at[g], {"dp": other})

    def got_w(b):
        return remote(w_row.at[b], w_row.at[b], w_send.at[0], w_recv.at[b], {"dp": b})

    def member(i):
        other = lax.rem(me + 1 + i, members)
        return other, {"mp": other // 2, "section": other % 2}

    def send_facts(i):
        return remote(facts.at[me], facts.at[me], fact_send.at[i], fact_recv.at[me], member(i)[1])

    def got_facts(i):
        other, target = member(i)
        return remote(facts.at[other], facts.at[other], fact_send.at[i], fact_recv.at[other], target)

    load_image = pltpu.make_async_copy(image_ref, cols.at[g, pl.ds(0, images)], load_sem.at[0])
    load_text = pltpu.make_async_copy(
        text_ref.at[:, pl.ds(pl.multiple_of(s * narrow, narrow), narrow)], staged, load_sem.at[1])
    load_image.start()
    load_text.start()

    barrier = pltpu.get_barrier_semaphore()

    def greet_member(i):
        pl.semaphore_signal(barrier, inc=1, device_id=member(i)[1], device_id_type=MESH)

    def greet_group(i):
        pl.semaphore_signal(
            barrier, inc=1, device_id={"dp": lax.rem(g + 1 + i, groups)}, device_id_type=MESH)

    loop(members - 1, greet_member)
    loop(groups - 1, greet_group)
    load_image.wait()
    pl.semaphore_wait(barrier, members + groups - 2)

    def send_own(c):
        pl.when(g < groups - 1)(lambda: to_right(g, c).start())
        pl.when(g > 0)(lambda: to_left(g, c).start())

    loop(images // CHUNK, send_own)
    loop(groups - 1, lambda i: send_code(i).start())

    code = code_ref[...]
    is_text = code < -1.5
    before = lax.broadcasted_iota(jnp.int32, (tokens, tokens), 0)
    after = lax.broadcasted_iota(jnp.int32, (tokens, tokens), 1)
    upto = (before <= after).astype(jnp.float32).astype(jnp.bfloat16)
    rank = jnp.dot(is_text.astype(jnp.float32).astype(jnp.bfloat16), upto,
                   preferred_element_type=jnp.float32)
    place = jnp.where(is_text, rank - 1.0, -1.0)[0:1, :]
    slot = lax.broadcasted_iota(jnp.int32, (texts, tokens), 0).astype(jnp.float32)
    pick = (slot == place).astype(jnp.float32).astype(jnp.bfloat16)
    load_text.wait()
    cols[g, pl.ds(images, texts), :] = jnp.dot(
        pick, staged[...], preferred_element_type=jnp.float32).astype(jnp.bfloat16)
    loop(texts // CHUNK, lambda c: send_own(c + images // CHUNK))

    def is_live(values):
        return ((values > -0.5) | ((values > -2.5) & (values < -1.5))).astype(jnp.float32)

    def squares(c):
        at = pl.multiple_of(c * LANES, LANES)
        x = cols[g, pl.ds(at, LANES), :].astype(jnp.float32)
        sums = jnp.sum(x * x, axis=1, keepdims=True)
        facts[me, :, pl.ds(at, LANES)] = jnp.transpose(
            jnp.broadcast_to(sums, (LANES, LANES)))[0:8, :]

    loop(tokens // LANES, squares)
    facts[me, :, pl.ds(tokens, narrow)] = gain_ref[...]
    loop(members - 1, lambda i: send_facts(i).start())

    row_contract = (((1,), (1,)), ((), ()))
    live_text = lax.dot_general(is_live(code).astype(jnp.bfloat16), pick, row_contract,
                                preferred_element_type=jnp.float32)
    codes[g] = code
    image_id = (lax.broadcasted_iota(jnp.int32, (images, tokens), 0) + g * images).astype(jnp.float32)
    ones = jnp.ones((8, tokens), jnp.bfloat16)
    live_image = jnp.zeros((8, images), jnp.float32)
    count = jnp.zeros((8, 1), jnp.float32)
    loop(groups - 1, lambda i: got_code(lax.rem(g + 1 + i, groups)).wait_recv())
    for b in range(groups):
        their = codes[b]
        found = (image_id == their[0:1, :]).astype(jnp.float32).astype(jnp.bfloat16)
        live_image += lax.dot_general(ones, found, row_contract, preferred_element_type=jnp.float32)
        count += jnp.sum(is_live(their), axis=1, keepdims=True)
    loop(members - 1, lambda i: got_facts(i).wait_recv())
    total = facts[0, :, pl.ds(0, tokens)]
    for d in range(1, members):
        total += facts[d, :, pl.ds(0, tokens)]
    factor = (2.0 / count) / (total / features + NORM_EPS)
    w_row[g, :, pl.ds(0, images)] = factor[:, :images] * live_image
    w_row[g, :, pl.ds(images, texts)] = factor[:, images:] * live_text
    loop(groups - 1, lambda i: send_w(i).start())
    for half in range(2):
        row_gain_ref[half] = facts[2 * g + half, :, pl.ds(tokens, narrow)]
    loop(groups - 1, lambda i: got_w(lax.rem(g + 1 + i, groups)).wait_recv())

    def turn_w(b):
        def part(c):
            at = pl.multiple_of(c * LANES, LANES)
            row = w_row[b, 0:1, pl.ds(at, LANES)]
            w_col[b, pl.ds(at, LANES), :] = jnp.transpose(jnp.broadcast_to(row, (LANES, LANES)))
        loop(tokens // LANES, part)

    loop(groups, turn_w)

    def clear(i):
        acc_ref[pl.ds(pl.multiple_of(i * TILE, TILE), TILE), :] = jnp.zeros((TILE, narrow), jnp.float32)

    loop(acc_ref.shape[0] // TILE, clear)
    gain_row = gain_ref[0:1, :]

    def multiply(b, at):
        at = pl.multiple_of(at, GROUP)
        x = cols[b, pl.ds(at, GROUP), :].astype(jnp.float32)
        scaled[...] = (x * w_col[b, pl.ds(at, GROUP), 0:1] * gain_row).astype(jnp.bfloat16)
        tiles = narrow // TILE

        def tile(i):
            half, lane = i // tiles, pl.multiple_of((i % tiles) * TILE, TILE)
            out = pl.ds(pl.multiple_of(i * TILE, TILE), TILE)
            acc_ref[out, :] += lax.dot_general(
                rows[half, b, pl.ds(at, GROUP), pl.ds(lane, TILE)], scaled[...],
                (((0,), (0,)), ((), ())), preferred_element_type=jnp.float32)

        loop(2 * tiles, tile)

    def step(t):
        j, c = t // per, t % per

        def each(side, act):
            b = g - j + 2 * j * side
            pl.when((b >= 0) & (b < groups) & ((j > 0) | (side == 0)))(lambda: act(b))

        def pass_on(side):
            def act(b):
                @pl.when(j > 0)
                def _():
                    to_right(b, c).wait_recv()
                    pl.when((side == 0) & (g < groups - 1))(lambda: to_right(b, c).start())
                    pl.when((side == 1) & (g > 0))(lambda: to_left(b, c).start())

            each(side, act)

        def share(side):
            def act(b):
                @pl.when(hop == 0)
                def _():
                    round_ring(cols, b, c).start()
                    to_sibling(cols, b, c, s).start()
                    keep_own(b, c).start()

                @pl.when(hop > 0)
                def _():
                    round_ring(cols, b, c).wait_recv()
                    pl.when(hop < 3)(lambda: round_ring(rows.at[s], b, c).start())
                    to_sibling(rows.at[s], b, c, s).start()

            each(side, act)

        def use(side):
            def act(b):
                to_sibling(cols, b, c, 1 - s).wait_recv()
                pl.when(hop == 0)(lambda: keep_own(b, c).wait())
                every = GROUP // CHUNK
                pl.when(c % every == every - 1)(lambda: multiply(b, (c // every) * GROUP))

            each(side, act)

        loop(2, pass_on)
        loop(2, share)
        loop(2, use)

    loop(groups * per, step)

    def finish(i):
        b, c = i // per, i % per
        pl.when((b <= g) & (g < groups - 1))(lambda: to_right(b, c).wait_send())
        pl.when((b >= g) & (g > 0))(lambda: to_left(b, c).wait_send())
        pl.when(hop < 3)(lambda: round_ring(cols, b, c).wait_send())
        to_sibling(cols, b, c, s).wait_send()

    loop(groups * per, finish)
    loop(groups - 1, lambda i: send_code(i).wait_send())
    loop(groups - 1, lambda i: send_w(i).wait_send())
    loop(members - 1, lambda i: send_facts(i).wait_send())


def ring_body(text_embeds, image_rows, image_source, live_len, norm_gain):
    groups = lax.axis_size("dp")
    members = lax.axis_size(("mp", "section"))
    tokens = text_embeds.shape[0]
    images, narrow = image_rows.shape
    live = jnp.arange(tokens, dtype=jnp.int32) < live_len[0]
    code = jnp.where(image_source >= 0, jnp.where(live, image_source, -1), jnp.where(live, -2, -3))
    code = jnp.broadcast_to(code.astype(jnp.float32)[None, :], (8, tokens))
    gain = jnp.broadcast_to(norm_gain.astype(jnp.float32)[None, :], (8, narrow))
    per = tokens // CHUNK
    dma = pltpu.SemaphoreType.DMA
    whole = pl.BlockSpec(memory_space=pltpu.VMEM)
    far = pl.BlockSpec(memory_space=pl.ANY)
    acc, row_gain = pl.pallas_call(
        functools.partial(hessian_kernel, groups),
        out_shape=(
            jax.ShapeDtypeStruct((2 * narrow, narrow), jnp.float32),
            jax.ShapeDtypeStruct((2, 8, narrow), jnp.float32),
        ),
        in_specs=[far, far, whole, whole],
        out_specs=(whole, whole),
        scratch_shapes=[
            pltpu.VMEM((groups, tokens, narrow), jnp.bfloat16),
            pltpu.VMEM((2, groups, tokens, narrow), jnp.bfloat16),
            pltpu.VMEM((tokens, narrow), jnp.bfloat16),
            pltpu.VMEM((groups, 8, tokens), jnp.float32),
            pltpu.VMEM((members, 8, tokens + narrow), jnp.float32),
            pltpu.VMEM((groups, 8, tokens), jnp.float32),
            pltpu.VMEM((groups, tokens, LANES), jnp.float32),
            pltpu.VMEM((GROUP, narrow), jnp.bfloat16),
            dma((2,)),
        ]
        + [dma((groups * per,)) for _ in range(8)]
        + [
            dma((groups,)), dma((groups,)), dma((members,)), dma((members,)),
            dma((groups,)), dma((groups,)),
        ],
        compiler_params=pltpu.CompilerParams(
            collective_id=0, has_side_effects=True, vmem_limit_bytes=56 * 1024 * 1024
        ),
    )(text_embeds, image_rows, code, gain)
    return acc * row_gain[:, 0, :].reshape(2 * narrow)[:, None]


def solution(mesh):
    in_specs = (P("dp", "mp"), P("dp", ("mp", "section")), P("dp"), P("dp"), P(("mp", "section")))
    out_specs = P("dp", ("mp", "section"))
    sizes = dict(mesh.shape)
    ringed = sizes["dp"] == 4 and sizes["mp"] == 4 and sizes["section"] == 2
    body = ring_body if ringed else general_body
    return jax.shard_map(body, mesh=mesh, in_specs=in_specs, out_specs=out_specs, check_vma=False)
```

```python
import functools

import jax
import jax.numpy as jnp
from jax import lax
from jax.experimental import pallas as pl
from jax.experimental.pallas import tpu as pltpu
from jax.sharding import PartitionSpec as P

NORM_EPS = 1e-06
MESH = pl.DeviceIdType.MESH
CHUNK = 64
GROUP = 256
LANES = 128
LATE = 4
TILE = 256


def general_body(text_embeds, image_rows, image_source, live_len, norm_gain):
    group_count = lax.axis_size("dp")
    feature_groups = lax.axis_size(("mp", "section"))
    tok_rows = text_embeds.shape[0]
    image_count = image_rows.shape[0]
    narrow = image_rows.shape[1]
    capacity = 2 * image_count // group_count
    section_part = lax.axis_index("section")
    own_text = lax.dynamic_slice_in_dim(text_embeds, section_part * narrow, narrow, 1)
    is_image = image_source >= 0
    safe_src = jnp.where(is_image, image_source, 0)
    owner_dev = safe_src // image_count
    local_row = safe_src % image_count
    peer_ids = jnp.arange(group_count, dtype=jnp.int32)
    onehot = ((owner_dev[:, None] == peer_ids[None, :]) & is_image[:, None]).astype(jnp.int32)
    slot_rank = jnp.sum(jnp.cumsum(onehot, axis=0) * onehot, axis=1) - 1
    empty_table = jnp.full((group_count * capacity,), -1, jnp.int32)
    wanted = jnp.where(is_image, owner_dev * capacity + slot_rank, group_count * capacity)
    request_table = empty_table.at[wanted].set(local_row, mode="drop")
    asked_rows = lax.all_to_all(
        request_table.reshape(group_count, capacity), "dp", split_axis=0, concat_axis=0, tiled=True
    )
    is_valid = asked_rows >= 0
    outgoing = image_rows[jnp.where(is_valid, asked_rows, 0)] * is_valid[:, :, None].astype(
        jnp.bfloat16
    )
    incoming = lax.all_to_all(outgoing, "dp", split_axis=0, concat_axis=0, tiled=True)
    wanted_slot = jnp.where(is_image, owner_dev * capacity + slot_rank, 0)
    picked = incoming.reshape(group_count * capacity, narrow)[wanted_slot]
    joined = jnp.where(is_image[:, None], picked, own_text)
    live_mask = (jnp.arange(tok_rows) < live_len[0]).astype(jnp.float32)[:, None]
    widened = joined.astype(jnp.float32)
    squares = lax.psum(jnp.sum(widened * widened, axis=1), ("mp", "section"))
    inverse = lax.rsqrt(squares / (narrow * feature_groups) + NORM_EPS)
    own_cols = (
        widened * inverse[:, None] * norm_gain.astype(jnp.float32)[None, :] * live_mask
    ).astype(jnp.bfloat16)
    contract = (((0,), (0,)), ((), ()))
    all_cols = lax.all_gather(own_cols, ("mp", "section"), axis=1, tiled=True)
    summed = lax.psum_scatter(
        lax.dot_general(all_cols, own_cols, contract, preferred_element_type=jnp.float32).astype(
            jnp.bfloat16
        ),
        "dp",
        scatter_dimension=0,
        tiled=True,
    ).astype(jnp.float32)
    live_count = lax.psum(jnp.sum(live_mask), "dp")
    return summed * (2.0 / live_count)


def ring_pos(m):
    y, x = m // 2, m % 2
    return y * (3 - x) + (1 - y) * x


def ring_chip(pos):
    y = pos // 2
    return 2 * y + (pos + y) % 2


def loop(count, step):
    lax.fori_loop(0, count, lambda i, carry: (step(i), carry)[1], 0)


def hessian_kernel(
    groups, text_ref, image_ref, code_ref, gain_ref, out_ref, row_gain_ref,
    acc_ref, cols, rows, staged, codes, facts, w_row, w_col, scaled,
    load_sem, right_send, left_send, z_recv, ring_send, ring_recv, sib_send, sib_recv, own_sem,
    code_send, code_recv, fact_send, fact_recv, w_send, w_recv,
):
    g, m, s = lax.axis_index("dp"), lax.axis_index("mp"), lax.axis_index("section")
    images, narrow = image_ref.shape
    tokens = cols.shape[1]
    texts = tokens - images
    per = tokens // CHUNK
    members = facts.shape[0]
    me = m * 2 + s
    features = members * narrow
    turn = 1 - 2 * s
    here = ring_pos(m)
    hop = ((here - ring_pos(g)) * turn + 4) % 4
    next_chip = ring_chip((here + turn + 4) % 4)

    def chunk(ref, b, c):
        return ref.at[b, pl.ds(pl.multiple_of(c * CHUNK, CHUNK), CHUNK)]

    def remote(src, dst, send, recv, target):
        return pltpu.make_async_remote_copy(
            src_ref=src, dst_ref=dst, send_sem=send, recv_sem=recv,
            device_id=target, device_id_type=MESH,
        )

    def to_right(b, c):
        return remote(chunk(cols, b, c), chunk(cols, b, c), right_send.at[b * per + c],
                      z_recv.at[b * per + c], {"dp": lax.rem(g + 1, groups)})

    def to_left(b, c):
        return remote(chunk(cols, b, c), chunk(cols, b, c), left_send.at[b * per + c],
                      z_recv.at[b * per + c], {"dp": lax.rem(g + groups - 1, groups)})

    def round_ring(src, b, c):
        return remote(chunk(src, b, c), chunk(rows.at[s], b, c), ring_send.at[b * per + c],
                      ring_recv.at[b * per + c], {"mp": next_chip})

    def to_sibling(src, b, c, half):
        return remote(chunk(src, b, c), chunk(rows.at[half], b, c), sib_send.at[b * per + c],
                      sib_recv.at[b * per + c], {"section": 1 - s})

    def keep_own(b, c):
        return pltpu.make_async_copy(
            chunk(cols, b, c), chunk(rows.at[s], b, c), own_sem.at[b * per + c])

    def send_code(i):
        other = lax.rem(g + 1 + i, groups)
        return remote(code_ref, codes.at[g], code_send.at[i], code_recv.at[g], {"dp": other})

    def got_code(b):
        return remote(code_ref, codes.at[b], code_send.at[0], code_recv.at[b], {"dp": b})

    def send_w(i):
        other = lax.rem(g + 1 + i, groups)
        return remote(w_row.at[g], w_row.at[g], w_send.at[i], w_recv.at[g], {"dp": other})

    def got_w(b):
        return remote(w_row.at[b], w_row.at[b], w_send.at[0], w_recv.at[b], {"dp": b})

    def member(i):
        other = lax.rem(me + 1 + i, members)
        return other, {"mp": other // 2, "section": other % 2}

    def send_facts(i):
        return remote(facts.at[me], facts.at[me], fact_send.at[i], fact_recv.at[me], member(i)[1])

    def got_facts(i):
        other, target = member(i)
        return remote(facts.at[other], facts.at[other], fact_send.at[i], fact_recv.at[other], target)

    load_image = pltpu.make_async_copy(image_ref, cols.at[g, pl.ds(0, images)], load_sem.at[0])
    load_text = pltpu.make_async_copy(
        text_ref.at[:, pl.ds(pl.multiple_of(s * narrow, narrow), narrow)], staged, load_sem.at[1])
    load_image.start()
    load_text.start()

    def clear(i):
        acc_ref[pl.ds(pl.multiple_of(i * TILE, TILE), TILE), :] = jnp.zeros((TILE, narrow), jnp.float32)

    barrier = pltpu.get_barrier_semaphore()

    def greet_member(i):
        pl.semaphore_signal(barrier, inc=1, device_id=member(i)[1], device_id_type=MESH)

    def greet_group(i):
        pl.semaphore_signal(
            barrier, inc=1, device_id={"dp": lax.rem(g + 1 + i, groups)}, device_id_type=MESH)

    loop(members - 1, greet_member)
    loop(groups - 1, greet_group)
    loop(acc_ref.shape[0] // TILE, clear)
    load_image.wait()
    pl.semaphore_wait(barrier, members + groups - 2)

    def send_own(c):
        pl.when(g < groups - 1)(lambda: to_right(g, c).start())
        pl.when(g > 0)(lambda: to_left(g, c).start())

    loop(groups - 1, lambda i: send_code(i).start())
    loop(images // CHUNK, send_own)

    code = code_ref[...]
    is_text = code < -1.5
    before = lax.broadcasted_iota(jnp.int32, (tokens, tokens), 0)
    after = lax.broadcasted_iota(jnp.int32, (tokens, tokens), 1)
    upto = (before <= after).astype(jnp.float32).astype(jnp.bfloat16)
    rank = jnp.dot(is_text.astype(jnp.float32).astype(jnp.bfloat16), upto,
                   preferred_element_type=jnp.float32)
    place = jnp.where(is_text, rank - 1.0, -1.0)[0:1, :]
    slot = lax.broadcasted_iota(jnp.int32, (texts, tokens), 0).astype(jnp.float32)
    pick = (slot == place).astype(jnp.float32).astype(jnp.bfloat16)
    load_text.wait()
    cols[g, pl.ds(images, texts), :] = jnp.dot(
        pick, staged[...], preferred_element_type=jnp.float32).astype(jnp.bfloat16)
    loop(texts // CHUNK, lambda c: send_own(c + images // CHUNK))

    def is_live(values):
        return ((values > -0.5) | ((values > -2.5) & (values < -1.5))).astype(jnp.float32)

    def squares(c):
        at = pl.multiple_of(c * LANES, LANES)
        x = cols[g, pl.ds(at, LANES), :].astype(jnp.float32)
        sums = jnp.sum(x * x, axis=1, keepdims=True)
        facts[me, :, pl.ds(at, LANES)] = jnp.transpose(
            jnp.broadcast_to(sums, (LANES, LANES)))[0:8, :]

    loop(tokens // LANES, squares)
    facts[me, :, pl.ds(tokens, narrow)] = gain_ref[...]
    loop(members - 1, lambda i: send_facts(i).start())

    row_contract = (((1,), (1,)), ((), ()))
    live_text = lax.dot_general(is_live(code).astype(jnp.bfloat16), pick, row_contract,
                                preferred_element_type=jnp.float32)
    codes[g] = code
    image_id = (lax.broadcasted_iota(jnp.int32, (images, tokens), 0) + g * images).astype(jnp.float32)
    ones = jnp.ones((8, tokens), jnp.bfloat16)
    live_image = jnp.zeros((8, images), jnp.float32)
    count = jnp.zeros((8, 1), jnp.float32)
    loop(groups - 1, lambda i: got_code(lax.rem(g + 1 + i, groups)).wait_recv())
    for b in range(groups):
        their = codes[b]
        found = (image_id == their[0:1, :]).astype(jnp.float32).astype(jnp.bfloat16)
        live_image += lax.dot_general(ones, found, row_contract, preferred_element_type=jnp.float32)
        count += jnp.sum(is_live(their), axis=1, keepdims=True)
    loop(members - 1, lambda i: got_facts(i).wait_recv())
    total = facts[0, :, pl.ds(0, tokens)]
    for d in range(1, members):
        total += facts[d, :, pl.ds(0, tokens)]
    factor = (2.0 / count) / (total / features + NORM_EPS)
    w_row[g, :, pl.ds(0, images)] = factor[:, :images] * live_image
    w_row[g, :, pl.ds(images, texts)] = factor[:, images:] * live_text
    loop(groups - 1, lambda i: send_w(i).start())
    for half in range(2):
        row_gain_ref[half] = facts[2 * g + half, :, pl.ds(tokens, narrow)]
    def turn_w(b):
        def part(c):
            at = pl.multiple_of(c * LANES, LANES)
            row = w_row[b, 0:1, pl.ds(at, LANES)]
            w_col[b, pl.ds(at, LANES), :] = jnp.transpose(jnp.broadcast_to(row, (LANES, LANES)))
        loop(tokens // LANES, part)

    turn_w(g)
    gain_row = gain_ref[0:1, :]
    every = GROUP // CHUNK
    sets = tokens // GROUP
    steps = every + (groups - 1) * per
    tiles = narrow // TILE
    share_tiles = 2 * tiles // every

    def each(t, act):
        @pl.when((t >= 0) & (t < every))
        def _():
            loop(sets, lambda e: act(e, g, e * every + t))

        @pl.when((t >= every) & (t < steps))
        def _():
            r = t - every

            def side(e):
                b = g + (2 * e - 1) * (1 + r // per)
                pl.when((b >= 0) & (b < groups))(lambda: act(e, b, r % per))

            loop(2, side)

    def pass_on(t):
        def act(e, b, c):
            @pl.when(t >= every)
            def _():
                to_right(b, c).wait_recv()
                pl.when((e == 0) & (g < groups - 1))(lambda: to_right(b, c).start())
                pl.when((e == 1) & (g > 0))(lambda: to_left(b, c).start())

            @pl.when(hop == 0)
            def _():
                round_ring(cols, b, c).start()
                to_sibling(cols, b, c, s).start()
                keep_own(b, c).start()

        each(t, act)

    def take_ring(t):
        def act(e, b, c):
            round_ring(cols, b, c).wait_recv()
            pl.when(hop < 3)(lambda: round_ring(rows.at[s], b, c).start())
            to_sibling(rows.at[s], b, c, s).start()

        pl.when(hop > 0)(lambda: each(t - hop, act))

    def take_sibling(t):
        def act(e, b, c):
            to_sibling(cols, b, c, 1 - s).wait_recv()
            pl.when(hop == 0)(lambda: keep_own(b, c).wait())

        each(t, act)

    def multiply(t):
        part = t % every

        def act(e, b, c):
            at = pl.multiple_of((c // every) * GROUP, GROUP)

            @pl.when((b != g) & (part == 0) & (c // every == 0))
            def _():
                got_w(b).wait_recv()
                turn_w(b)

            @pl.when(part == 0)
            def _():
                x = cols[b, pl.ds(at, GROUP), :].astype(jnp.float32)
                scaled[e] = (x * w_col[b, pl.ds(at, GROUP), 0:1] * gain_row).astype(jnp.bfloat16)

            def tile(n):
                i = part * share_tiles + n
                half, lane = i // tiles, pl.multiple_of((i % tiles) * TILE, TILE)
                out = pl.ds(pl.multiple_of(i * TILE, TILE), TILE)
                acc_ref[out, :] += lax.dot_general(
                    rows[half, b, pl.ds(at, GROUP), pl.ds(lane, TILE)], scaled[e],
                    (((0,), (0,)), ((), ())), preferred_element_type=jnp.float32)

            loop(share_tiles, tile)

        each(t, act)

    def step(t):
        pass_on(t)
        take_ring(t)
        take_sibling(t - LATE)
        multiply(t - LATE - every)

    loop(steps + LATE + every, step)

    def write(i):
        part = pl.ds(pl.multiple_of(i * TILE, TILE), TILE)
        out_ref[part, :] = acc_ref[part, :].astype(out_ref.dtype)

    loop(acc_ref.shape[0] // TILE, write)

    def finish(i):
        b, c = i // per, i % per
        pl.when((b <= g) & (g < groups - 1))(lambda: to_right(b, c).wait_send())
        pl.when((b >= g) & (g > 0))(lambda: to_left(b, c).wait_send())
        pl.when(hop < 3)(lambda: round_ring(cols, b, c).wait_send())
        to_sibling(cols, b, c, s).wait_send()

    loop(groups * per, finish)
    loop(groups - 1, lambda i: send_code(i).wait_send())
    loop(groups - 1, lambda i: send_w(i).wait_send())
    loop(members - 1, lambda i: send_facts(i).wait_send())


def ring_body(text_embeds, image_rows, image_source, live_len, norm_gain):
    groups = lax.axis_size("dp")
    members = lax.axis_size(("mp", "section"))
    tokens = text_embeds.shape[0]
    images, narrow = image_rows.shape
    live = jnp.arange(tokens, dtype=jnp.int32) < live_len[0]
    code = jnp.where(image_source >= 0, jnp.where(live, image_source, -1), jnp.where(live, -2, -3))
    code = jnp.broadcast_to(code.astype(jnp.float32)[None, :], (8, tokens))
    gain = jnp.broadcast_to(norm_gain.astype(jnp.float32)[None, :], (8, narrow))
    per = tokens // CHUNK
    dma = pltpu.SemaphoreType.DMA
    whole = pl.BlockSpec(memory_space=pltpu.VMEM)
    far = pl.BlockSpec(memory_space=pl.ANY)
    acc, row_gain = pl.pallas_call(
        functools.partial(hessian_kernel, groups),
        out_shape=(
            jax.ShapeDtypeStruct((2 * narrow, narrow), jnp.bfloat16),
            jax.ShapeDtypeStruct((2, 8, narrow), jnp.float32),
        ),
        in_specs=[far, far, whole, whole],
        out_specs=(whole, whole),
        scratch_shapes=[
            pltpu.VMEM((2 * narrow, narrow), jnp.float32),
            pltpu.VMEM((groups, tokens, narrow), jnp.bfloat16),
            pltpu.VMEM((2, groups, tokens, narrow), jnp.bfloat16),
            pltpu.VMEM((tokens, narrow), jnp.bfloat16),
            pltpu.VMEM((groups, 8, tokens), jnp.float32),
            pltpu.VMEM((members, 8, tokens + narrow), jnp.float32),
            pltpu.VMEM((groups, 8, tokens), jnp.float32),
            pltpu.VMEM((groups, tokens, LANES), jnp.float32),
            pltpu.VMEM((tokens // GROUP, GROUP, narrow), jnp.bfloat16),
            dma((2,)),
        ]
        + [dma((groups * per,)) for _ in range(8)]
        + [
            dma((groups,)), dma((groups,)), dma((members,)), dma((members,)),
            dma((groups,)), dma((groups,)),
        ],
        compiler_params=pltpu.CompilerParams(
            collective_id=0, has_side_effects=True, vmem_limit_bytes=40 * 1024 * 1024
        ),
    )(text_embeds, image_rows, code, gain)
    return acc.astype(jnp.float32) * row_gain[:, 0, :].reshape(2 * narrow)[:, None]


def solution(mesh):
    in_specs = (P("dp", "mp"), P("dp", ("mp", "section")), P("dp"), P("dp"), P(("mp", "section")))
    out_specs = P("dp", ("mp", "section"))
    sizes = dict(mesh.shape)
    ringed = sizes["dp"] == 4 and sizes["mp"] == 4 and sizes["section"] == 2
    body = ring_body if ringed else general_body
    return jax.shard_map(body, mesh=mesh, in_specs=in_specs, out_specs=out_specs, check_vma=False)
```

```python
import functools

import jax
import jax.numpy as jnp
from jax import lax
from jax.experimental import pallas as pl
from jax.experimental.pallas import tpu as pltpu
from jax.sharding import PartitionSpec as P

NORM_EPS = 1e-06
MESH = pl.DeviceIdType.MESH
CHUNK = 64
GROUP = 256
LANES = 128
AHEAD = 2
TILE = 256


def general_body(text_embeds, image_rows, image_source, live_len, norm_gain):
    group_count = lax.axis_size("dp")
    feature_groups = lax.axis_size(("mp", "section"))
    tok_rows = text_embeds.shape[0]
    image_count = image_rows.shape[0]
    narrow = image_rows.shape[1]
    capacity = 2 * image_count // group_count
    section_part = lax.axis_index("section")
    own_text = lax.dynamic_slice_in_dim(text_embeds, section_part * narrow, narrow, 1)
    is_image = image_source >= 0
    safe_src = jnp.where(is_image, image_source, 0)
    owner_dev = safe_src // image_count
    local_row = safe_src % image_count
    peer_ids = jnp.arange(group_count, dtype=jnp.int32)
    onehot = ((owner_dev[:, None] == peer_ids[None, :]) & is_image[:, None]).astype(jnp.int32)
    slot_rank = jnp.sum(jnp.cumsum(onehot, axis=0) * onehot, axis=1) - 1
    empty_table = jnp.full((group_count * capacity,), -1, jnp.int32)
    wanted = jnp.where(is_image, owner_dev * capacity + slot_rank, group_count * capacity)
    request_table = empty_table.at[wanted].set(local_row, mode="drop")
    asked_rows = lax.all_to_all(
        request_table.reshape(group_count, capacity), "dp", split_axis=0, concat_axis=0, tiled=True
    )
    is_valid = asked_rows >= 0
    outgoing = image_rows[jnp.where(is_valid, asked_rows, 0)] * is_valid[:, :, None].astype(
        jnp.bfloat16
    )
    incoming = lax.all_to_all(outgoing, "dp", split_axis=0, concat_axis=0, tiled=True)
    wanted_slot = jnp.where(is_image, owner_dev * capacity + slot_rank, 0)
    picked = incoming.reshape(group_count * capacity, narrow)[wanted_slot]
    joined = jnp.where(is_image[:, None], picked, own_text)
    live_mask = (jnp.arange(tok_rows) < live_len[0]).astype(jnp.float32)[:, None]
    widened = joined.astype(jnp.float32)
    squares = lax.psum(jnp.sum(widened * widened, axis=1), ("mp", "section"))
    inverse = lax.rsqrt(squares / (narrow * feature_groups) + NORM_EPS)
    own_cols = (
        widened * inverse[:, None] * norm_gain.astype(jnp.float32)[None, :] * live_mask
    ).astype(jnp.bfloat16)
    contract = (((0,), (0,)), ((), ()))
    all_cols = lax.all_gather(own_cols, ("mp", "section"), axis=1, tiled=True)
    summed = lax.psum_scatter(
        lax.dot_general(all_cols, own_cols, contract, preferred_element_type=jnp.float32).astype(
            jnp.bfloat16
        ),
        "dp",
        scatter_dimension=0,
        tiled=True,
    ).astype(jnp.float32)
    live_count = lax.psum(jnp.sum(live_mask), "dp")
    return summed * (2.0 / live_count)


def ring_pos(m):
    y, x = m // 2, m % 2
    return y * (3 - x) + (1 - y) * x


def ring_chip(pos):
    y = pos // 2
    return 2 * y + (pos + y) % 2


def loop(count, step):
    lax.fori_loop(0, count, lambda i, carry: (step(i), carry)[1], 0)


def hessian_kernel(
    groups, text_ref, image_ref, code_ref, gain_ref, out_ref, row_gain_ref,
    acc_ref, cols, rows, staged, codes, facts, w_row, w_col, scaled,
    load_sem, right_send, left_send, z_recv, ring_send, back_send, ring_recv, sib_send, sib_recv, own_sem,
    code_send, code_recv, fact_send, fact_recv, w_send, w_recv,
):
    g, m, s = lax.axis_index("dp"), lax.axis_index("mp"), lax.axis_index("section")
    images, narrow = image_ref.shape
    tokens = cols.shape[1]
    texts = tokens - images
    per = tokens // CHUNK
    members = facts.shape[0]
    me = m * 2 + s
    features = members * narrow
    turn = 1 - 2 * s
    here = ring_pos(m)
    hop = ((here - ring_pos(g)) * turn + 4) % 4
    next_chip = ring_chip((here + turn + 4) % 4)
    back_chip = ring_chip((here - turn + 4) % 4)
    every = GROUP // CHUNK
    sib_lag = (4 - hop) % 4 + 1 + (3 - hop) // 3
    lead_lag = hop - hop // 3

    def chunk(ref, b, c):
        return ref.at[b, pl.ds(pl.multiple_of(c * CHUNK, CHUNK), CHUNK)]

    def remote(src, dst, send, recv, target):
        return pltpu.make_async_remote_copy(
            src_ref=src, dst_ref=dst, send_sem=send, recv_sem=recv,
            device_id=target, device_id_type=MESH,
        )

    def to_right(b, c):
        return remote(chunk(cols, b, c), chunk(cols, b, c), right_send.at[b * per + c],
                      z_recv.at[b * per + c], {"dp": lax.rem(g + 1, groups)})

    def to_left(b, c):
        return remote(chunk(cols, b, c), chunk(cols, b, c), left_send.at[b * per + c],
                      z_recv.at[b * per + c], {"dp": lax.rem(g + groups - 1, groups)})

    def round_ring(src, b, c):
        return remote(chunk(src, b, c), chunk(rows.at[s], b, c), ring_send.at[b * per + c],
                      ring_recv.at[b * per + c], {"mp": next_chip})

    def is_last(b, c):
        return ((b - g) * (b - g) == (groups - 1) * (groups - 1)) & (c >= per - every)

    def ring_back(b, c):
        return remote(chunk(cols, b, c), chunk(rows.at[s], b, c), back_send.at[c - (per - every)],
                      ring_recv.at[b * per + c], {"mp": back_chip})

    def to_sibling(src, b, c, half):
        return remote(chunk(src, b, c), chunk(rows.at[half], b, c), sib_send.at[b * per + c],
                      sib_recv.at[b * per + c], {"section": 1 - s})

    def keep_own(b, c):
        return pltpu.make_async_copy(
            chunk(cols, b, c), chunk(rows.at[s], b, c), own_sem.at[b * per + c])

    def send_code(i):
        other = lax.rem(g + 1 + i, groups)
        return remote(code_ref.at[pl.ds(0, 1)], codes.at[g, pl.ds(0, 1)], code_send.at[i], code_recv.at[g], {"dp": other})

    def got_code(b):
        return remote(code_ref.at[pl.ds(0, 1)], codes.at[b, pl.ds(0, 1)], code_send.at[0], code_recv.at[b], {"dp": b})

    def send_w(i):
        other = lax.rem(g + 1 + i, groups)
        return remote(w_row.at[g, pl.ds(0, 1)], w_row.at[g, pl.ds(0, 1)], w_send.at[i], w_recv.at[g], {"dp": other})

    def got_w(b):
        return remote(w_row.at[b, pl.ds(0, 1)], w_row.at[b, pl.ds(0, 1)], w_send.at[0], w_recv.at[b], {"dp": b})

    def member(i):
        other = lax.rem(me + 1 + i, members)
        return other, {"mp": other // 2, "section": other % 2}

    def send_facts(i):
        return remote(facts.at[me, pl.ds(0, 1)], facts.at[me, pl.ds(0, 1)], fact_send.at[i], fact_recv.at[me], member(i)[1])

    def got_facts(i):
        other, target = member(i)
        return remote(facts.at[other, pl.ds(0, 1)], facts.at[other, pl.ds(0, 1)], fact_send.at[i],
                      fact_recv.at[other], target)

    load_image = pltpu.make_async_copy(image_ref, cols.at[g, pl.ds(0, images)], load_sem.at[0])
    load_text = pltpu.make_async_copy(
        text_ref.at[:, pl.ds(pl.multiple_of(s * narrow, narrow), narrow)], staged, load_sem.at[1])
    load_image.start()
    load_text.start()

    def clear(i):
        acc_ref[pl.ds(pl.multiple_of(i * TILE, TILE), TILE), :] = jnp.zeros((TILE, narrow), jnp.float32)

    barrier = pltpu.get_barrier_semaphore()

    def greet_member(i):
        pl.semaphore_signal(barrier, inc=1, device_id=member(i)[1], device_id_type=MESH)

    def greet_group(i):
        pl.semaphore_signal(
            barrier, inc=1, device_id={"dp": lax.rem(g + 1 + i, groups)}, device_id_type=MESH)

    loop(members - 1, greet_member)
    loop(groups - 1, greet_group)
    loop(acc_ref.shape[0] // TILE, clear)
    load_image.wait()
    pl.semaphore_wait(barrier, members + groups - 2)

    def send_own(c):
        pl.when(g < groups - 1)(lambda: to_right(g, c).start())
        pl.when(g > 0)(lambda: to_left(g, c).start())

    loop(groups - 1, lambda i: send_code(i).start())
    loop(images // CHUNK, send_own)

    code = code_ref[...]
    is_text = code < -1.5
    before = lax.broadcasted_iota(jnp.int32, (tokens, tokens), 0)
    after = lax.broadcasted_iota(jnp.int32, (tokens, tokens), 1)
    upto = (before <= after).astype(jnp.float32).astype(jnp.bfloat16)
    rank = jnp.dot(is_text.astype(jnp.float32).astype(jnp.bfloat16), upto,
                   preferred_element_type=jnp.float32)
    place = jnp.where(is_text, rank - 1.0, -1.0)[0:1, :]
    slot = lax.broadcasted_iota(jnp.int32, (texts, tokens), 0).astype(jnp.float32)
    pick = (slot == place).astype(jnp.float32).astype(jnp.bfloat16)
    load_text.wait()
    cols[g, pl.ds(images, texts), :] = jnp.dot(
        pick, staged[...], preferred_element_type=jnp.float32).astype(jnp.bfloat16)
    loop(AHEAD, lambda c: send_own(c + images // CHUNK))

    def is_live(values):
        return ((values > -0.5) | ((values > -2.5) & (values < -1.5))).astype(jnp.float32)

    def squares(c):
        at = pl.multiple_of(c * LANES, LANES)
        x = cols[g, pl.ds(at, LANES), :].astype(jnp.float32)
        sums = jnp.sum(x * x, axis=1, keepdims=True)
        facts[me, 0:1, pl.ds(at, LANES)] = jnp.transpose(
            jnp.broadcast_to(sums, (LANES, LANES)))[0:1, :]

    loop(tokens // LANES, squares)
    facts[me, 0:1, pl.ds(tokens, narrow)] = gain_ref[0:1, :]
    loop(members - 1, lambda i: send_facts(i).start())

    row_contract = (((1,), (1,)), ((), ()))
    live_text = lax.dot_general(is_live(code).astype(jnp.bfloat16), pick, row_contract,
                                preferred_element_type=jnp.float32)
    codes[g, 0:1, :] = code[0:1, :]
    image_id = (lax.broadcasted_iota(jnp.int32, (images, tokens), 0) + g * images).astype(jnp.float32)
    ones = jnp.ones((8, tokens), jnp.bfloat16)
    live_image = jnp.zeros((8, images), jnp.float32)
    count = jnp.zeros((1, 1), jnp.float32)
    loop(groups - 1, lambda i: got_code(lax.rem(g + 1 + i, groups)).wait_recv())
    for b in range(groups):
        their = codes[b, 0:1, :]
        found = (image_id == their).astype(jnp.float32).astype(jnp.bfloat16)
        live_image += lax.dot_general(ones, found, row_contract, preferred_element_type=jnp.float32)
        count += jnp.sum(is_live(their), axis=1, keepdims=True)
    loop(members - 1, lambda i: got_facts(i).wait_recv())
    total = facts[0, 0:1, pl.ds(0, tokens)]
    for d in range(1, members):
        total += facts[d, 0:1, pl.ds(0, tokens)]
    factor = (2.0 / count) / (total / features + NORM_EPS)
    w_row[g, 0:1, pl.ds(0, images)] = factor[:, :images] * live_image[0:1, :]
    w_row[g, 0:1, pl.ds(images, texts)] = factor[:, images:] * live_text[0:1, :]
    loop(groups - 1, lambda i: send_w(i).start())
    loop(texts // CHUNK - AHEAD, lambda c: send_own(c + images // CHUNK + AHEAD))
    for half in range(2):
        row_gain_ref[half] = jnp.broadcast_to(
            facts[2 * g + half, 0:1, pl.ds(tokens, narrow)], (8, narrow))
    def turn_w(b):
        def part(c):
            at = pl.multiple_of(c * LANES, LANES)
            row = w_row[b, 0:1, pl.ds(at, LANES)]
            w_col[b, pl.ds(at, LANES), :] = jnp.transpose(jnp.broadcast_to(row, (LANES, LANES)))
        loop(tokens // LANES, part)

    turn_w(g)
    gain_row = gain_ref[0:1, :]
    sets = tokens // GROUP
    steps = every + (groups - 1) * per
    tiles = narrow // TILE
    share_tiles = tiles // every

    def each(t, act):
        @pl.when((t >= 0) & (t < every))
        def _():
            loop(sets, lambda e: act(e, g, e * every + t))

        @pl.when((t >= every) & (t < steps))
        def _():
            r = t - every

            def side(e):
                b = g + (2 * e - 1) * (1 + r // per)
                pl.when((b >= 0) & (b < groups))(lambda: act(e, b, r % per))

            loop(2, side)

    def pass_on(t):
        def act(e, b, c):
            @pl.when(t >= every)
            def _():
                to_right(b, c).wait_recv()
                pl.when((e == 0) & (g < groups - 1))(lambda: to_right(b, c).start())
                pl.when((e == 1) & (g > 0))(lambda: to_left(b, c).start())

            @pl.when(hop == 0)
            def _():
                round_ring(cols, b, c).start()
                pl.when(is_last(b, c))(lambda: ring_back(b, c).start())
                to_sibling(cols, b, c, s).start()
                keep_own(b, c).start()

        each(t, act)

    def take_ring(t):
        def act(e, b, c):
            round_ring(cols, b, c).wait_recv()
            pl.when((hop == 1) | ((hop == 2) & ~is_last(b, c)))(
                lambda: round_ring(rows.at[s], b, c).start())
            to_sibling(rows.at[s], b, c, s).start()

        pl.when(hop > 0)(lambda: each(t - hop, act))

    def take_sibling(t):
        def act(e, b, c):
            to_sibling(cols, b, c, 1 - s).wait_recv()

        each(t, act)

    def weigh(t):
        def act(e, b, c):
            at = pl.multiple_of((c // every) * GROUP, GROUP)

            @pl.when((b != g) & (c == 0))
            def _():
                got_w(b).wait_recv()
                turn_w(b)

            x = cols[b, pl.ds(at, GROUP), :].astype(jnp.float32)
            scaled[(t // every) % 2 * sets + e] = (
                x * w_col[b, pl.ds(at, GROUP), 0:1] * gain_row).astype(jnp.bfloat16)

        pl.when((t >= 0) & (t % every == 0))(lambda: each(t, act))

    def multiply(t, half):
        def act(e, b, c):
            at = pl.multiple_of((c // every) * GROUP, GROUP)

            def tile(n):
                i = (t % every) * share_tiles + n
                out = pl.ds(pl.multiple_of(half * narrow + i * TILE, TILE), TILE)
                value = acc_ref[out, :] + lax.dot_general(
                    rows[half, b, pl.ds(at, GROUP), pl.ds(pl.multiple_of(i * TILE, TILE), TILE)],
                    scaled[(t // every) % 2 * sets + e],
                    (((0,), (0,)), ((), ())), preferred_element_type=jnp.float32)
                acc_ref[out, :] = value

                @pl.when(t >= steps - every)
                def _():
                    out_ref[out, :] = value.astype(out_ref.dtype)

            loop(share_tiles, tile)

        each(t, act)

    def step(t):
        pass_on(t)
        take_ring(t)
        pl.when(hop == 0)(lambda: each(t - 1, lambda e, b, c: keep_own(b, c).wait()))
        take_sibling(t - sib_lag)
        weigh(t - lead_lag - every)
        multiply(t - hop - every, s)
        multiply(t - sib_lag - every, 1 - s)

    loop(steps + 4 + every, step)

    @pl.when((g > 0) & (g < groups - 1))
    def _():
        def write(i):
            part = pl.ds(pl.multiple_of(i * TILE, TILE), TILE)
            out_ref[part, :] = acc_ref[part, :].astype(out_ref.dtype)

        loop(acc_ref.shape[0] // TILE, write)

    def finish(i):
        b, c = i // per, i % per
        pl.when((b <= g) & (g < groups - 1))(lambda: to_right(b, c).wait_send())
        pl.when((b >= g) & (g > 0))(lambda: to_left(b, c).wait_send())
        pl.when((hop < 2) | ((hop == 2) & ~is_last(b, c)))(
            lambda: round_ring(cols, b, c).wait_send())
        pl.when((hop == 0) & is_last(b, c))(lambda: ring_back(b, c).wait_send())
        to_sibling(cols, b, c, s).wait_send()

    loop(groups * per, finish)
    loop(groups - 1, lambda i: send_code(i).wait_send())
    loop(groups - 1, lambda i: send_w(i).wait_send())
    loop(members - 1, lambda i: send_facts(i).wait_send())


def ring_body(text_embeds, image_rows, image_source, live_len, norm_gain):
    groups = lax.axis_size("dp")
    members = lax.axis_size(("mp", "section"))
    tokens = text_embeds.shape[0]
    images, narrow = image_rows.shape
    live = jnp.arange(tokens, dtype=jnp.int32) < live_len[0]
    code = jnp.where(image_source >= 0, jnp.where(live, image_source, -1), jnp.where(live, -2, -3))
    code = jnp.broadcast_to(code.astype(jnp.float32)[None, :], (8, tokens))
    gain = jnp.broadcast_to(norm_gain.astype(jnp.float32)[None, :], (8, narrow))
    per = tokens // CHUNK
    dma = pltpu.SemaphoreType.DMA
    whole = pl.BlockSpec(memory_space=pltpu.VMEM)
    far = pl.BlockSpec(memory_space=pl.ANY)
    acc, row_gain = pl.pallas_call(
        functools.partial(hessian_kernel, groups),
        out_shape=(
            jax.ShapeDtypeStruct((2 * narrow, narrow), jnp.bfloat16),
            jax.ShapeDtypeStruct((2, 8, narrow), jnp.float32),
        ),
        in_specs=[far, far, whole, whole],
        out_specs=(whole, whole),
        scratch_shapes=[
            pltpu.VMEM((2 * narrow, narrow), jnp.float32),
            pltpu.VMEM((groups, tokens, narrow), jnp.bfloat16),
            pltpu.VMEM((2, groups, tokens, narrow), jnp.bfloat16),
            pltpu.VMEM((tokens, narrow), jnp.bfloat16),
            pltpu.VMEM((groups, 8, tokens), jnp.float32),
            pltpu.VMEM((members, 8, tokens + narrow), jnp.float32),
            pltpu.VMEM((groups, 8, tokens), jnp.float32),
            pltpu.VMEM((groups, tokens, LANES), jnp.float32),
            pltpu.VMEM((2 * (tokens // GROUP), GROUP, narrow), jnp.bfloat16),
            dma((2,)),
        ]
        + [dma((groups * per,)) for _ in range(4)]
        + [dma((GROUP // CHUNK,))]
        + [dma((groups * per,)) for _ in range(4)]
        + [
            dma((groups,)), dma((groups,)), dma((members,)), dma((members,)),
            dma((groups,)), dma((groups,)),
        ],
        compiler_params=pltpu.CompilerParams(
            collective_id=0, has_side_effects=True, vmem_limit_bytes=40 * 1024 * 1024
        ),
    )(text_embeds, image_rows, code, gain)
    return acc.astype(jnp.float32) * row_gain[:, 0, :].reshape(2 * narrow)[:, None]


def solution(mesh):
    in_specs = (P("dp", "mp"), P("dp", ("mp", "section")), P("dp"), P("dp"), P(("mp", "section")))
    out_specs = P("dp", ("mp", "section"))
    sizes = dict(mesh.shape)
    ringed = sizes["dp"] == 4 and sizes["mp"] == 4 and sizes["section"] == 2
    body = ring_body if ringed else general_body
    return jax.shard_map(body, mesh=mesh, in_specs=in_specs, out_specs=out_specs, check_vma=False)
```
